32 devices in a mesh: seq: 8 (over y, x, core), tp: 4 (over z).
Axes of the slice: x: 2, y: 2, z: 4, core: 2. Of those that a mesh axis runs over, the one named last changes fastest.
Arguments:
- tokens: bfloat16 [7168, 8192], P('seq', 'tp'), may hold values from -500 to 500
- query_tokens: bfloat16 [512, 8192], P('seq', 'tp'), may hold values from -500 to 500
- norm_gain: float32 [8192], replicated, may hold values from 0.1 to 1.9
- w_query: bfloat16 [8192, 4096], P(None, 'tp'), may hold values from -0.125 to 0.125
- w_key: bfloat16 [8192, 512], P('seq', 'tp'), may hold values from -0.0625 to 0.0625
- w_value: bfloat16 [8192, 512], P('seq', 'tp'), may hold values from -0.25 to 0.25
- cache_key: bfloat16 [1536, 512], P('seq', 'tp'), may hold values from -122 to 122
- cache_value: bfloat16 [1536, 512], P('seq', 'tp'), may hold values from -24 to 24
- seg_lengths: int32 [56], replicated, may hold values from 0 to 128, as said below
- prompt_query: int32 [56], replicated, may hold values from 0 to 7
- query_lengths: int32 [8], replicated, may hold values from 16 to 64
- assignment: int32 [56], replicated, may hold values from -1 to 31, as said below
Outputs:
- block_out: bfloat16 [4096, 4096], P('seq', 'tp')
- query_out: bfloat16 [512, 4096], P('seq', 'tp')
The draws below stay inside these ranges and needn't reach their ends.
Inputs may be any that keep to these rules, and one draw needn't show every extreme that they name: `seg_lengths`: A slot without a passage has length 0, a live one 128 // 3 to 128. The live slots of a device come first. A device and the device half the seq axis away hold 8 live slots together, one of them 4 or more; some device holds 7. `assignment`: -1 exactly for the slots of length 0; the live slots carry the prompt positions 0 to 31, each once, and position p belongs to device p // 4. A live slot's position belongs to its own device or to the device half the seq axis away; every device gives at least one and at most 4 positions of that other device, and in every draw some device gives 4.
All inputs are finite; a program needn't handle non-finite values.
Results may differ from the reference program's by a relative error of at most 0.014.
The reference program's roundings to bfloat16 on the way count: a program that leaves them out, or rounds other values in their place, can miss the bound.
Values may be sent and summed in bfloat16 or wider, within the bound.
A program may use at most 128 MiB of HBM per device.

```python
import math
import jax
import jax.numpy as jnp
from jax import lax

D = 8192
HEADS = 32
KV_HEADS = 4
HEAD_DIM = 128
BLK = 128
INSTR = 1536
QLEN = 64
BAL = 4
SLOTS = 7
PROMPTS = 32
NQ = 8
N_SEQ = 8


def layout_plan(key):
    plan_key = jax.random.fold_in(key, 7001)
    keys_list = jax.random.split(plan_key, 6)
    seq_count = PROMPTS // BAL
    half_count = seq_count // 2
    flips = jax.random.randint(keys_list[0], (half_count,), 0, 2).astype(jnp.int32)
    shifts = jax.random.randint(keys_list[1], (half_count,), 0, BAL).astype(jnp.int32)
    shifts = shifts.at[0].set(BAL - 1)
    mutual = jax.random.randint(keys_list[5], (half_count,), 1, BAL - shifts + 1).astype(jnp.int32)
    pair_ids = jnp.arange(half_count, dtype=jnp.int32)
    heavy = pair_ids + flips * half_count
    light = pair_ids + (1 - flips) * half_count
    counts = jnp.zeros((seq_count,), jnp.int32)
    counts = counts.at[heavy].set(BAL + shifts)
    counts = counts.at[light].set(BAL - shifts)
    device_ids = jnp.arange(seq_count, dtype=jnp.int32)
    pair_of = device_ids % half_count
    is_heavy = counts > BAL
    is_heavy = is_heavy | (shifts[pair_of] == 0) & (flips[pair_of] * half_count == device_ids - pair_of)
    kept = jnp.where(is_heavy, BAL - mutual[pair_of], BAL - shifts[pair_of] - mutual[pair_of]).astype(jnp.int32)
    partner = (device_ids + half_count) % seq_count
    slot_ids = jnp.arange(SLOTS, dtype=jnp.int32)
    live_slots = slot_ids[None, :] < counts[:, None]
    lengths = jax.random.randint(keys_list[2], (seq_count, SLOTS), BLK // 3, BLK + 1).astype(jnp.int32)
    lengths = jnp.where(live_slots, lengths, 0).reshape(-1)
    slot_orders = jax.vmap(lambda one_key: jax.random.permutation(one_key, SLOTS))(jax.random.split(keys_list[3], seq_count)).astype(jnp.int32)
    before = live_slots[:, None, :] & (slot_orders[:, None, :] < slot_orders[:, :, None])
    ranks = jnp.sum(before.astype(jnp.int32), axis=2).astype(jnp.int32)
    staying = ranks < kept[:, None]
    dest_device = jnp.where(staying, device_ids[:, None], partner[:, None]).astype(jnp.int32)
    dest_index = jnp.where(staying, ranks, kept[partner][:, None] + ranks - kept[:, None])
    dest_index = jnp.clip(dest_index, 0, BAL - 1).astype(jnp.int32)
    orders = jax.vmap(lambda one_key: jax.random.permutation(one_key, BAL))(jax.random.split(keys_list[4], seq_count)).astype(jnp.int32)
    dest_slot = orders[dest_device, dest_index]
    assigned = jnp.where(live_slots, dest_device * BAL + dest_slot, -1).reshape(-1)
    return (lengths.astype(jnp.int32), assigned.astype(jnp.int32))


def draw_seg_lengths(key, part):
    return layout_plan(key)[0]


def draw_assignment(key, part):
    return layout_plan(key)[1]


def feature_rows(key, row_count, salt):
    draw_key = jax.random.fold_in(key, salt)
    scale_key, column_key, noise_key = jax.random.split(draw_key, 3)
    row_scale = jnp.exp(jax.random.uniform(scale_key, (row_count, 1), jnp.float32, 0.0, math.log(10.0)))
    column_scale = jnp.exp(jax.random.uniform(column_key, (1, D), jnp.float32, 0.0, math.log(10.0)))
    noise = jnp.clip(jax.random.normal(noise_key, (row_count, D), jnp.float32), -5.0, 5.0)
    return (noise * row_scale * column_scale).astype(jnp.bfloat16)


def draw_tokens(key, part):
    return feature_rows(key, PROMPTS // BAL * SLOTS * BLK, 11)


def draw_query_tokens(key, part):
    return feature_rows(key, NQ * QLEN, 13)


def draw_cache_key(key, part):
    draw_key = jax.random.fold_in(key, 17)
    drawn_key = jax.random.fold_in(draw_key, 0)
    width = KV_HEADS * HEAD_DIM
    drawn = jnp.clip(jax.random.normal(drawn_key, (INSTR, width), jnp.float32), -6.0, 6.0)
    return drawn.astype(jnp.bfloat16)


def touch_ends(result, own_key, low, high):
    shape = result.shape
    spot = [jax.random.randint(jax.random.fold_in(own_key, axis), (), 0, shape[axis]) for axis in range(len(shape))]
    result = result.at[tuple(spot)].set(low)
    longest = shape.index(max(shape))
    spot[longest] = (spot[longest] + 1) % shape[longest]
    return result.at[tuple(spot)].set(high)


def block_scale(stream_key, shape, shards, smallest, high):
    gain = 1.0
    for axis_at, shards_of in shards:
        draws = jax.random.uniform(jax.random.fold_in(jax.random.fold_in(stream_key, 6), axis_at), (shards_of,), jnp.float32, smallest / len(shards), high / len(shards))
        gain = gain * jnp.repeat(jnp.exp(draws), shape[axis_at] // shards_of).reshape((-1,) + (1,) * (len(shape) - 1 - axis_at))
    return gain


def gaussian(own_key, shape, deviation, most, cuts=(), held_as=jnp.bfloat16):
    level = block_scale(own_key, shape, cuts, -0.22, 0.18) if cuts else 1.0
    array = jax.random.normal(own_key, shape, jnp.float32) * deviation * level
    return jnp.minimum(jnp.maximum(array, -most), most).astype(held_as)


def setup_inputs(seed: int = 0) -> dict:
    splits = jax.random.split(jax.random.key(seed), 13)
    tokens = draw_tokens(jax.random.fold_in(splits[12], 71), 0)
    query_tokens = draw_query_tokens(jax.random.fold_in(splits[12], 71), 0)
    norm_gain = jnp.clip(1.0 + 0.18 * jax.random.normal(splits[2], (D,), jnp.float32), 0.1, 1.9)
    w_query = gaussian(splits[3], (D, HEADS * HEAD_DIM), (D // 4) ** -0.5, 0.125, ((1, 4),))
    w_key = gaussian(splits[4], (D, KV_HEADS * HEAD_DIM), D ** -0.5, 0.0625, ((0, 8), (1, 4)))
    w_value = gaussian(splits[5], (D, KV_HEADS * HEAD_DIM), (D // 16) ** -0.5, 0.25, ((0, 8), (1, 4)))
    cache_key = draw_cache_key(jax.random.fold_in(splits[12], 71), 0)
    cache_value = gaussian(splits[7], (INSTR, KV_HEADS * HEAD_DIM), 4.0, 24.0, ((0, 8), (1, 4)))
    seg_lengths = draw_seg_lengths(jax.random.fold_in(splits[12], 71), 0)
    prompt_query = touch_ends(jax.random.randint(splits[9], (N_SEQ * SLOTS,), 0, NQ), jax.random.fold_in(splits[9], 1), 0, NQ - 1).astype(jnp.int32)
    query_lengths = touch_ends(jax.random.randint(splits[10], (NQ,), QLEN // 4, QLEN + 1), jax.random.fold_in(splits[10], 1), QLEN // 4, QLEN).astype(jnp.int32)
    assignment = draw_assignment(jax.random.fold_in(splits[12], 71), 0)
    return {"tokens": tokens, "query_tokens": query_tokens, "norm_gain": norm_gain, "w_query": w_query, "w_key": w_key, "w_value": w_value, "cache_key": cache_key, "cache_value": cache_value, "seg_lengths": seg_lengths, "prompt_query": prompt_query, "query_lengths": query_lengths, "assignment": assignment}


eps_norm = 1e-05
rope_base = 500000.0
masked_score = -1e+30

def normalize(row_block, norm_gain):
    values = row_block.astype(jnp.float32)
    mean_square = lax.optimization_barrier(jnp.mean(values * values, axis=-1, keepdims=True))
    return (values * lax.rsqrt(mean_square + eps_norm) * norm_gain).astype(jnp.bfloat16)

def rotate(values, positions):
    half_width = values.shape[-1] // 2
    exponent = jnp.arange(half_width, dtype=jnp.float32) * (2.0 / values.shape[-1])
    inverse = jnp.power(jnp.float32(rope_base), -exponent)
    angle = positions.astype(jnp.float32)[:, None] * inverse[None, :]
    cosine = jnp.cos(angle)[:, None, :]
    sine_part = jnp.sin(angle)[:, None, :]
    first_half = values[..., :half_width]
    second_half = values[..., half_width:]
    return jnp.concatenate([first_half * cosine - second_half * sine_part, second_half * cosine + first_half * sine_part], axis=-1)

def attend(queries, keys_all, values_all, visible, live_rows):
    score_scale = 1.0 / math.sqrt(queries.shape[-1])
    scores = jnp.einsum('rhgd,khd->hgrk', queries.astype(jnp.float32), keys_all.astype(jnp.float32)) * score_scale
    scores = jnp.where(visible[None, None], scores, masked_score)
    largest = lax.optimization_barrier(jnp.max(scores, axis=-1, keepdims=True))
    powers = jnp.exp(scores - largest)
    weights = (powers / lax.optimization_barrier(jnp.sum(powers, axis=-1, keepdims=True))).astype(jnp.bfloat16)
    mixed = jnp.einsum('hgrk,khd->rhgd', weights.astype(jnp.float32), values_all.astype(jnp.float32))
    mixed = jnp.where(live_rows[:, None, None, None], mixed, 0.0)
    return mixed.reshape(queries.shape[0], -1).astype(jnp.bfloat16)

def reference(tokens, query_tokens, norm_gain, w_query, w_key, w_value, cache_key, cache_value, seg_lengths, prompt_query, query_lengths, assignment):
    group_size = HEADS // KV_HEADS
    all_slots = N_SEQ * SLOTS
    targets = jnp.arange(PROMPTS, dtype=jnp.int32)
    matches = assignment[None, :] == targets[:, None]
    slot_index = jnp.arange(all_slots, dtype=jnp.int32)
    sources = lax.optimization_barrier(jnp.sum(jnp.where(matches, slot_index[None, :], 0), axis=1)).astype(jnp.int32)
    lengths = seg_lengths[sources]
    prompt_queries = prompt_query[sources]
    prompt_offsets = query_lengths[prompt_queries]
    source_blocks = tokens.reshape(all_slots, BLK, D)
    cache_keys = cache_key.reshape(INSTR, KV_HEADS, HEAD_DIM)
    cache_values = cache_value.reshape(INSTR, KV_HEADS, HEAD_DIM)
    query_normed = normalize(query_tokens, norm_gain)
    query_positions = INSTR + jnp.arange(QLEN, dtype=jnp.int32)
    text_queries = jnp.dot(query_normed, w_query, preferred_element_type=jnp.float32).reshape(NQ, QLEN, HEADS, HEAD_DIM)
    text_keys = jnp.dot(query_normed, w_key, preferred_element_type=jnp.float32).reshape(NQ, QLEN, KV_HEADS, HEAD_DIM)
    text_values = jnp.dot(query_normed, w_value, preferred_element_type=jnp.float32).reshape(NQ, QLEN, KV_HEADS, HEAD_DIM)
    text_queries = jax.vmap(lambda one_query: rotate(one_query, query_positions))(text_queries).astype(jnp.bfloat16)
    text_keys = jax.vmap(lambda one_query: rotate(one_query, query_positions))(text_keys).astype(jnp.bfloat16)
    text_values = text_values.astype(jnp.bfloat16)
    query_rows = jnp.arange(QLEN, dtype=jnp.int32)
    block_rows = jnp.arange(BLK, dtype=jnp.int32)

    def query_step(query_index):
        text_length = query_lengths[query_index]
        keys_all = jnp.concatenate([cache_keys, text_keys[query_index]], axis=0)
        values_all = jnp.concatenate([cache_values, text_values[query_index]], axis=0)
        causal = (query_rows[None, :] <= query_rows[:, None]) & (query_rows[None, :] < text_length)
        visible = jnp.concatenate([jnp.ones((QLEN, INSTR), dtype=bool), causal], axis=1)
        grouped = text_queries[query_index].reshape(QLEN, KV_HEADS, group_size, HEAD_DIM)
        return attend(grouped, keys_all, values_all, visible, query_rows < text_length)
    query_out = lax.map(query_step, jnp.arange(NQ, dtype=jnp.int32)).reshape(NQ * QLEN, HEADS * HEAD_DIM)
    passage_causal = block_rows[None, :] <= block_rows[:, None]

    def block_step(position):
        source = sources[position]
        normed = normalize(source_blocks[source], norm_gain)
        queries = jnp.dot(normed, w_query, preferred_element_type=jnp.float32).reshape(BLK, HEADS, HEAD_DIM)
        passage_keys = jnp.dot(normed, w_key, preferred_element_type=jnp.float32).reshape(BLK, KV_HEADS, HEAD_DIM)
        passage_values = jnp.dot(normed, w_value, preferred_element_type=jnp.float32).reshape(BLK, KV_HEADS, HEAD_DIM)
        offset = prompt_offsets[position]
        positions = INSTR + offset + block_rows
        queries = rotate(queries, positions).astype(jnp.bfloat16)
        passage_keys = rotate(passage_keys, positions).astype(jnp.bfloat16)
        passage_values = passage_values.astype(jnp.bfloat16)
        owner_query = prompt_queries[position]
        keys_all = jnp.concatenate([cache_keys, text_keys[owner_query], passage_keys], axis=0)
        values_all = jnp.concatenate([cache_values, text_values[owner_query], passage_values], axis=0)
        visible = jnp.concatenate([jnp.ones((BLK, INSTR), dtype=bool), jnp.broadcast_to(query_rows[None, :] < offset, (BLK, QLEN)), passage_causal], axis=1)
        grouped = queries.reshape(BLK, KV_HEADS, group_size, HEAD_DIM)
        return attend(grouped, keys_all, values_all, visible, block_rows < lengths[position])
    block_out = lax.map(block_step, targets).reshape(PROMPTS * BLK, HEADS * HEAD_DIM)
    return (block_out, query_out)
```

```python
import math

import jax
import jax.numpy as jnp
from jax import lax
from jax.sharding import PartitionSpec as P

HEAD_DIM = 128
BLK = 128
INSTR = 1536
QLEN = 64
BAL = 4


eps_norm = 1e-05
rope_base = 500000.0
masked_score = -1e30


def passed_along(block, axis, distance):
    devices = range(lax.axis_size(axis))
    route = [((i - distance) % len(devices), i) for i in devices]
    return lax.ppermute(block, axis, route)


def rotate(values, positions):
    half_width = values.shape[-1] // 2
    exponent = jnp.arange(half_width, dtype=jnp.float32) * (2.0 / values.shape[-1])
    inverse = jnp.power(jnp.float32(rope_base), -exponent)
    angle = positions.astype(jnp.float32)[:, None] * inverse[None, :]
    cosine = jnp.cos(angle)[:, None, :]
    sine_part = jnp.sin(angle)[:, None, :]
    first_half = values[..., :half_width]
    second_half = values[..., half_width:]
    return jnp.concatenate(
        [
            first_half * cosine - second_half * sine_part,
            second_half * cosine + first_half * sine_part,
        ],
        axis=-1,
    )


def attend(queries, keys_all, values_all, visible, live_rows):
    score_scale = 1.0 / math.sqrt(queries.shape[-1])
    scores = (
        jnp.einsum("rhgd,khd->hgrk", queries, keys_all, preferred_element_type=jnp.float32)
        * score_scale
    )
    scores = jnp.where(visible[None, None], scores, masked_score)
    largest = jnp.max(scores, axis=-1, keepdims=True)
    powers = jnp.exp(scores - largest)
    weights = (powers / jnp.sum(powers, axis=-1, keepdims=True)).astype(jnp.bfloat16)
    mixed = jnp.einsum("hgrk,khd->rhgd", weights, values_all, preferred_element_type=jnp.float32)
    mixed = jnp.where(live_rows[:, None, None, None], mixed, 0.0)
    return mixed.reshape(queries.shape[0], -1).astype(jnp.bfloat16)


def matmul(left, right):
    return jnp.dot(left, right, preferred_element_type=jnp.float32)


def gather_rows(block, axis):
    count = lax.axis_size(axis)
    if count & (count - 1):
        return lax.all_gather(block, axis, axis=0, tiled=False)
    index = lax.axis_index(axis)
    held = block[None]
    bit = count // 2
    while bit:
        route = [(i, i ^ bit) for i in range(count)]
        other = lax.ppermute(held, axis, route)
        high = (index & bit) != 0
        held = jnp.stack([jnp.where(high, other, held), jnp.where(high, held, other)], axis=1)
        held = held.reshape((-1,) + block.shape)
        bit //= 2
    return held


def after(value, earlier):
    return lax.optimization_barrier((value, earlier))


def body(
    tokens,
    query_tokens,
    norm_gain,
    w_query,
    w_key,
    w_value,
    cache_key,
    cache_value,
    seg_lengths,
    prompt_query,
    query_lengths,
    assignment,
):
    seq_count = lax.axis_size("seq")
    device = lax.axis_index("seq")
    kv_local = w_key.shape[1] // HEAD_DIM
    heads_local = w_query.shape[1] // HEAD_DIM
    group_size = heads_local // kv_local
    local_queries = query_tokens.shape[0] // QLEN
    half_axis = seq_count // 2
    partner = (device + half_axis) % seq_count
    slots = tokens.shape[0] // BLK
    slot_ids = jnp.arange(assignment.shape[0], dtype=jnp.int32)
    my_lengths = lax.dynamic_slice_in_dim(query_lengths, device * local_queries, local_queries)
    query_cols = jnp.arange(QLEN, dtype=jnp.int32)
    passage_rows = jnp.arange(BLK, dtype=jnp.int32)

    def of_position(position, table):
        return jnp.sum(jnp.where(assignment == position, table, 0))

    def local_block(position):
        slot = of_position(position, slot_ids) - device * slots
        mine = (slot >= 0) & (slot < slots)
        start = jnp.clip(slot, 0, slots - 1) * BLK
        return mine, lax.dynamic_slice_in_dim(tokens, start, BLK, axis=0)

    def all_features(rows):
        gathered = lax.all_gather(rows, "tp", axis=0, tiled=False)
        values = gathered.astype(jnp.float32)
        gains = norm_gain.reshape(gathered.shape[0], 1, -1)
        mean_square = jnp.mean(values * values, axis=(0, 2), keepdims=True)
        normed = (values * lax.rsqrt(mean_square + eps_norm) * gains).astype(jnp.bfloat16)
        return normed.transpose(1, 0, 2).reshape(rows.shape[0], -1)

    full_query = all_features(query_tokens)

    packed = jnp.concatenate([w_key, w_value, cache_key, cache_value], axis=0)
    incoming = []
    shared = None
    for c in range(BAL):
        block = local_block(partner * BAL + c)[1]
        if c == 1:
            packed, incoming[0] = after(packed, incoming[0])
            shared = gather_rows(packed, "seq")
        if c:
            block, incoming[-1] = after(block, incoming[-1])
        incoming.append(passed_along(block, "seq", half_axis))
    blocks = []
    for c in range(BAL):
        mine, kept = local_block(device * BAL + c)
        blocks.append(jnp.where(mine, kept, incoming[c]))

    depth, cache_depth = w_key.shape[0], cache_key.shape[0]
    width = w_key.shape[1]
    w_both = jnp.concatenate([shared[:, :depth], shared[:, depth : 2 * depth]], axis=2)
    w_both = w_both.reshape(-1, 2 * width)
    cache_keys = shared[:, 2 * depth : 2 * depth + cache_depth].reshape(-1, kv_local, HEAD_DIM)
    cache_values = shared[:, 2 * depth + cache_depth :].reshape(-1, kv_local, HEAD_DIM)
    cache_rows = cache_keys.shape[0]

    def project(normed, positions):
        rows = normed.shape[0]
        queries = matmul(normed, w_query).reshape(rows, heads_local, HEAD_DIM)
        both = matmul(normed, w_both)
        queries = rotate(queries, positions).astype(jnp.bfloat16)
        keys = rotate(both[:, :width].reshape(rows, kv_local, HEAD_DIM), positions)
        values = both[:, width:].reshape(rows, kv_local, HEAD_DIM)
        return (
            queries.reshape(rows, kv_local, group_size, HEAD_DIM),
            keys.astype(jnp.bfloat16),
            values.astype(jnp.bfloat16),
        )

    text_positions = jnp.tile(INSTR + query_cols, local_queries)
    text_q, text_k, text_v = project(full_query, text_positions)
    text_all = gather_rows(jnp.stack([text_k, text_v]), "seq")
    text_all = text_all.reshape(seq_count, 2, local_queries, QLEN, kv_local, HEAD_DIM)

    query_out = []
    for n in range(local_queries):
        rows = slice(n * QLEN, (n + 1) * QLEN)
        keys_all = jnp.concatenate([cache_keys, text_k[rows]], axis=0)
        values_all = jnp.concatenate([cache_values, text_v[rows]], axis=0)
        length = my_lengths[n]
        causal = (query_cols[None, :] <= query_cols[:, None]) & (query_cols[None, :] < length)
        visible = jnp.concatenate([jnp.ones((QLEN, cache_rows), dtype=bool), causal], axis=1)
        query_out.append(attend(text_q[rows], keys_all, values_all, visible, query_cols < length))
    query_out = jnp.concatenate(query_out, axis=0)

    passage_causal = passage_rows[None, :] <= passage_rows[:, None]
    block_out = []
    for c in range(BAL):
        position = device * BAL + c
        length = of_position(position, seg_lengths)
        owner = of_position(position, prompt_query)
        offset = lax.dynamic_index_in_dim(query_lengths, owner, 0, keepdims=False)
        queries, keys, values = project(all_features(blocks[c]), INSTR + offset + passage_rows)
        text = lax.dynamic_slice(
            text_all,
            (owner // local_queries, 0, owner % local_queries, 0, 0, 0),
            (1, 2, 1) + text_all.shape[3:],
        )[0, :, 0]
        visible = jnp.concatenate(
            [
                jnp.ones((BLK, cache_rows), dtype=bool),
                jnp.broadcast_to(query_cols[None, :] < offset, (BLK, QLEN)),
                passage_causal,
            ],
            axis=1,
        )
        block_out.append(
            attend(
                queries,
                jnp.concatenate([cache_keys, text[0], keys], axis=0),
                jnp.concatenate([cache_values, text[1], values], axis=0),
                visible,
                passage_rows < length,
            )
        )
    return (jnp.concatenate(block_out, axis=0), query_out)


def solution(mesh):
    placed = (
        P("seq", "tp"),
        P("seq", "tp"),
        P(),
        P(None, "tp"),
        P("seq", "tp"),
        P("seq", "tp"),
        P("seq", "tp"),
        P("seq", "tp"),
        P(),
        P(),
        P(),
        P(),
    )
    return jax.shard_map(
        body,
        mesh=mesh,
        in_specs=placed,
        out_specs=(P("seq", "tp"), P("seq", "tp")),
        check_vma=False,
    )
```

```python
import math

import jax
import jax.numpy as jnp
from jax import lax
from jax.sharding import PartitionSpec as P

HEAD_DIM = 128
BLK = 128
INSTR = 1536
QLEN = 64
BAL = 4


eps_norm = 1e-05
rope_base = 500000.0
masked_score = -1e30


def passed_along(block, axis, distance):
    devices = range(lax.axis_size(axis))
    route = [((i - distance) % len(devices), i) for i in devices]
    return lax.ppermute(block, axis, route)


def rotate(values, positions):
    half_width = values.shape[-1] // 2
    exponent = jnp.arange(half_width, dtype=jnp.float32) * (2.0 / values.shape[-1])
    inverse = jnp.power(jnp.float32(rope_base), -exponent)
    angle = positions.astype(jnp.float32)[:, None] * inverse[None, :]
    cosine = jnp.cos(angle)[:, None, :]
    sine_part = jnp.sin(angle)[:, None, :]
    first_half = values[..., :half_width]
    second_half = values[..., half_width:]
    return jnp.concatenate(
        [
            first_half * cosine - second_half * sine_part,
            second_half * cosine + first_half * sine_part,
        ],
        axis=-1,
    )


def attend(queries, keys_all, values_all, visible, live_rows):
    score_scale = 1.0 / math.sqrt(queries.shape[-1])
    scores = (
        jnp.einsum("rhgd,khd->hgrk", queries, keys_all, preferred_element_type=jnp.float32)
        * score_scale
    )
    scores = jnp.where(visible[None, None], scores, masked_score)
    largest = jnp.max(scores, axis=-1, keepdims=True)
    powers = jnp.exp(scores - largest)
    weights = (powers / jnp.sum(powers, axis=-1, keepdims=True)).astype(jnp.bfloat16)
    mixed = jnp.einsum("hgrk,khd->rhgd", weights, values_all, preferred_element_type=jnp.float32)
    mixed = jnp.where(live_rows[:, None, None, None], mixed, 0.0)
    return mixed.reshape(queries.shape[0], -1).astype(jnp.bfloat16)


def matmul(left, right):
    return jnp.dot(left, right, preferred_element_type=jnp.float32)


def gather_rows(block, axis):
    count = lax.axis_size(axis)
    if count & (count - 1):
        return lax.all_gather(block, axis, axis=0, tiled=False)
    index = lax.axis_index(axis)
    held = block[None]
    places = jnp.zeros((count,), jnp.int32)
    apart = jnp.arange(count, dtype=jnp.int32) ^ index
    bit, width = count // 2, 1
    while bit:
        other = lax.ppermute(held, axis, [(i, i ^ bit) for i in range(count)])
        held = jnp.concatenate([held, other], axis=0)
        places = places + jnp.where((apart & bit) != 0, width, 0)
        bit, width = bit // 2, width * 2
    return jnp.concatenate(
        [lax.dynamic_slice_in_dim(held, places[n], 1, axis=0) for n in range(count)], axis=0
    )


def after(value, earlier):
    return lax.optimization_barrier((value, earlier))


def body(
    tokens,
    query_tokens,
    norm_gain,
    w_query,
    w_key,
    w_value,
    cache_key,
    cache_value,
    seg_lengths,
    prompt_query,
    query_lengths,
    assignment,
):
    seq_count = lax.axis_size("seq")
    device = lax.axis_index("seq")
    kv_local = w_key.shape[1] // HEAD_DIM
    heads_local = w_query.shape[1] // HEAD_DIM
    group_size = heads_local // kv_local
    local_queries = query_tokens.shape[0] // QLEN
    half_axis = seq_count // 2
    partner = (device + half_axis) % seq_count
    slots = tokens.shape[0] // BLK
    slot_ids = jnp.arange(assignment.shape[0], dtype=jnp.int32)
    my_lengths = lax.dynamic_slice_in_dim(query_lengths, device * local_queries, local_queries)
    query_cols = jnp.arange(QLEN, dtype=jnp.int32)
    passage_rows = jnp.arange(BLK, dtype=jnp.int32)

    def of_position(position, table):
        return jnp.sum(jnp.where(assignment == position, table, 0))

    def local_block(position):
        slot = of_position(position, slot_ids) - device * slots
        mine = (slot >= 0) & (slot < slots)
        start = jnp.clip(slot, 0, slots - 1) * BLK
        return mine, lax.dynamic_slice_in_dim(tokens, start, BLK, axis=0)

    def normed_rows(gathered):
        values = gathered.astype(jnp.float32)
        gains = norm_gain.reshape(gathered.shape[0], 1, -1)
        mean_square = jnp.mean(values * values, axis=(0, 2), keepdims=True)
        normed = (values * lax.rsqrt(mean_square + eps_norm) * gains).astype(jnp.bfloat16)
        return normed.transpose(1, 0, 2).reshape(gathered.shape[1], -1)

    def all_features(rows):
        return lax.all_gather(rows, "tp", axis=0, tiled=False)

    full_query = normed_rows(all_features(query_tokens))

    packed = jnp.concatenate([w_key, w_value, cache_key, cache_value], axis=0)
    incoming = []
    shared = None
    for c in range(BAL):
        block = local_block(partner * BAL + c)[1]
        if c == 1:
            packed, incoming[0] = after(packed, incoming[0])
            shared = gather_rows(packed, "seq")
        if c:
            block, incoming[-1] = after(block, incoming[-1])
        incoming.append(passed_along(block, "seq", half_axis))
    blocks = []
    for c in range(BAL):
        mine, kept = local_block(device * BAL + c)
        blocks.append(jnp.where(mine, kept, incoming[c]))

    depth, cache_depth = w_key.shape[0], cache_key.shape[0]
    width = w_key.shape[1]
    w_both = jnp.concatenate([shared[:, :depth], shared[:, depth : 2 * depth]], axis=2)
    w_both = w_both.reshape(-1, 2 * width)
    cache_keys = shared[:, 2 * depth : 2 * depth + cache_depth].reshape(-1, kv_local, HEAD_DIM)
    cache_values = shared[:, 2 * depth + cache_depth :].reshape(-1, kv_local, HEAD_DIM)
    cache_rows = cache_keys.shape[0]

    def project(normed, positions):
        rows = normed.shape[0]
        queries = matmul(normed, w_query).reshape(rows, heads_local, HEAD_DIM)
        both = matmul(normed, w_both)
        queries = rotate(queries, positions).astype(jnp.bfloat16)
        keys = rotate(both[:, :width].reshape(rows, kv_local, HEAD_DIM), positions)
        values = both[:, width:].reshape(rows, kv_local, HEAD_DIM)
        return (
            queries.reshape(rows, kv_local, group_size, HEAD_DIM),
            keys.astype(jnp.bfloat16),
            values.astype(jnp.bfloat16),
        )

    text_positions = jnp.tile(INSTR + query_cols, local_queries)
    text_q, text_k, text_v = project(full_query, text_positions)
    text_all = gather_rows(jnp.stack([text_k, text_v]), "seq")
    text_all = text_all.reshape(seq_count, 2, local_queries, QLEN, kv_local, HEAD_DIM)

    query_out = []
    for n in range(local_queries):
        rows = slice(n * QLEN, (n + 1) * QLEN)
        keys_all = jnp.concatenate([cache_keys, text_k[rows]], axis=0)
        values_all = jnp.concatenate([cache_values, text_v[rows]], axis=0)
        length = my_lengths[n]
        causal = (query_cols[None, :] <= query_cols[:, None]) & (query_cols[None, :] < length)
        visible = jnp.concatenate([jnp.ones((QLEN, cache_rows), dtype=bool), causal], axis=1)
        query_out.append(attend(text_q[rows], keys_all, values_all, visible, query_cols < length))
    query_out = jnp.concatenate(query_out, axis=0)

    passage_causal = passage_rows[None, :] <= passage_rows[:, None]
    block_out = []
    for c in range(BAL):
        position = device * BAL + c
        length = of_position(position, seg_lengths)
        owner = of_position(position, prompt_query)
        offset = lax.dynamic_index_in_dim(query_lengths, owner, 0, keepdims=False)
        rows = blocks[c]
        if c >= 2:
            rows, block_out[c - 2] = after(rows, block_out[c - 2])
        gathered = all_features(rows)
        if c:
            gathered, block_out[c - 1] = after(gathered, block_out[c - 1])
        queries, keys, values = project(normed_rows(gathered), INSTR + offset + passage_rows)
        text = lax.dynamic_slice(
            text_all,
            (owner // local_queries, 0, owner % local_queries, 0, 0, 0),
            (1, 2, 1) + text_all.shape[3:],
        )[0, :, 0]
        visible = jnp.concatenate(
            [
                jnp.ones((BLK, cache_rows), dtype=bool),
                jnp.broadcast_to(query_cols[None, :] < offset, (BLK, QLEN)),
                passage_causal,
            ],
            axis=1,
        )
        block_out.append(
            attend(
                queries,
                jnp.concatenate([cache_keys, text[0], keys], axis=0),
                jnp.concatenate([cache_values, text[1], values], axis=0),
                visible,
                passage_rows < length,
            )
        )
    return (jnp.concatenate(block_out, axis=0), query_out)


def solution(mesh):
    placed = (
        P("seq", "tp"),
        P("seq", "tp"),
        P(),
        P(None, "tp"),
        P("seq", "tp"),
        P("seq", "tp"),
        P("seq", "tp"),
        P("seq", "tp"),
        P(),
        P(),
        P(),
        P(),
    )
    return jax.shard_map(
        body,
        mesh=mesh,
        in_specs=placed,
        out_specs=(P("seq", "tp"), P("seq", "tp")),
        check_vma=False,
    )
```
